32 devices in a mesh: region: 2 (over y), tx: 4 (over z), ty: 2 (over x), band: 2 (over core).
Axes of the slice: x: 2, y: 2, z: 4, core: 2. Of those that a mesh axis runs over, the one named last changes fastest.
Arguments:
- scenes: bfloat16 [4, 256, 12, 256], P(('region', 'ty'), 'tx', 'band'), parts along dimension 0, may hold values from -6 to 6
- cloud: bfloat16 [4, 256, 256], P(('region', 'ty'), 'tx'), parts along dimension 0, may hold values from 0.049804688 to 1
- destination: int32 [4, 256], P(('region', 'ty'), 'tx'), parts along dimension 0, may hold values from 0 to 3, as said below
- offset: int32 [4, 256], P(('region', 'ty'), 'tx'), parts along dimension 0, may hold values from 0 to 63
- counts: int32 [4, 4], P(('region', 'ty'), 'tx'), parts along dimension 0, may hold values from 32 to 64
Outputs:
- composite: bfloat16 [12, 4, 128, 512], P('band', ('region', 'ty'), 'tx'), parts along dimension 1
The draws below stay inside these ranges and needn't reach their ends.
There are 2 independent parts, one for each index of `region`. The reference program is written for one: setup_inputs(seed, part) draws one part's arguments, and reference() takes and returns one part's arrays. A program takes and returns all parts, laid end to end along the dimension named above; each array names one. Nothing has to cross between parts.
Inputs may be any that keep to these rules, and one draw needn't show every extreme that they name: `destination`: among the 64 blocks of one device no tile row is named more than 32 times, and the first 32 blocks of every device in one column of tiles name one common tile row. `offset`: slots are numbered row by row, 8 slots to a row. A device's first counts blocks are live; its other blocks add nothing.
All inputs are finite; a program needn't handle non-finite values.
Results may differ from the reference program's by a relative error of at most 0.0025.
Values may be sent and summed in bfloat16 or wider, within the bound.
A program may use at most 64 MiB of HBM per device.

```python
import math
import jax
import jax.numpy as jnp
from jax import lax

BANDS = 12
TS = 128
BS = 16
S_DEV = 64
LEVELS = 4
CAP = 32
SLOTS = 64
NR = 512
NC = 256
N_TX = 4
N_TY = 2


def draw_destination(key, part):
    folded = jax.random.fold_in(key, 7)
    key_star, key_rest = jax.random.split(folded)
    hot_rows = jax.random.randint(key_star, (N_TY,), 0, N_TX)
    hot_each = jnp.repeat(hot_rows, N_TX)
    subkeys = jax.random.split(key_rest, N_TY * N_TX)

    def one_device(subkey, hot_row):
        others = jnp.arange((N_TX - 1) * CAP, dtype=jnp.int32) // CAP
        others = others + (others >= hot_row).astype(jnp.int32)
        mixed = jax.random.permutation(subkey, others)
        leading = jnp.full((CAP,), hot_row, jnp.int32)
        return jnp.concatenate([leading, mixed[:S_DEV - CAP]])
    table = jax.vmap(one_device)(subkeys, hot_each)
    return table.reshape(N_TY, N_TX * S_DEV).astype(jnp.int32)


def plant(array, key, least, high):
    index_at = [jax.random.randint(jax.random.fold_in(key, axis), (), 0, length) for axis, length in enumerate(array.shape)]
    longest = array.shape.index(max(array.shape))
    beside = index_at[:longest] + [(index_at[longest] + 1) % array.shape[longest]] + index_at[longest + 1:]
    return array.at[tuple(index_at)].set(least).at[tuple(beside)].set(high)


def shard_levels(stream_key, shape, cuts, least, largest):
    loudness, own = 1.0, jax.random.fold_in(stream_key, 6)
    for axis_at, blocks in cuts:
        steps = jnp.exp(jax.random.uniform(jax.random.fold_in(own, axis_at), (blocks,), jnp.float32, least / len(cuts), largest / len(cuts)))
        loudness = loudness * jnp.repeat(steps, shape[axis_at] // blocks).reshape([-1 if axis == axis_at else 1 for axis in range(len(shape))])
    return loudness


def normal_values(rng, shape, scale, bound, cuts=(), held_as=jnp.bfloat16):
    array = scale * jax.random.normal(rng, shape, jnp.float32)
    if cuts:
        array = array * shard_levels(rng, shape, cuts, -0.22, 0.18)
    return jnp.clip(array, -bound, bound).astype(held_as)


def setup_inputs(seed: int = 0, part: int = 0) -> dict:
    seeds = jax.random.split(jax.random.key(seed), 6)
    own_keys = jax.random.split(jax.random.fold_in(seeds[5], part), 6)
    return {
        "scenes": normal_values(own_keys[0], (N_TY, N_TX * S_DEV, BANDS, BS * BS), 1.0, 6.0, ((0, 2), (1, 4), (2, 2))),
        "cloud": jnp.clip(jnp.exp(math.log(1.0) - 2.9996462 * jax.random.uniform(own_keys[1], (N_TY, N_TX * S_DEV, BS * BS), jnp.float32) ** shard_levels(own_keys[1], (N_TY, N_TX * S_DEV, BS * BS), ((0, 2), (1, 4)), -0.2, 0.2)), 0.049804688, 1.0).astype(jnp.bfloat16),
        "destination": draw_destination(jax.random.fold_in(jax.random.fold_in(seeds[5], part), 71), part),
        "offset": plant(jax.random.randint(own_keys[3], (N_TY, N_TX * S_DEV), 0, SLOTS), jax.random.fold_in(own_keys[3], 1), 0, SLOTS - 1).astype(jnp.int32),
        "counts": plant(jax.random.randint(own_keys[4], (N_TY, N_TX), CAP, S_DEV + 1), jax.random.fold_in(own_keys[4], 1), CAP, S_DEV).astype(jnp.int32),
    }


BINOMIAL = (0.0625, 0.25, 0.375, 0.25, 0.0625)
BACKGROUND = 0.25


def shrink_axis(field, along, rim_in, rim_out):
    length = field.shape[along]
    extent = length - 2 * rim_in
    outputs = extent // 2 + 2 * rim_out
    first_index = rim_in - 2 - 2 * rim_out
    running = None
    for tap_index, tap_weight in enumerate(BINOMIAL):
        begin = first_index + tap_index
        piece = lax.slice_in_dim(field, begin, begin + 2 * (outputs - 1) + 1, 2, along)
        running = tap_weight * piece if running is None else running + tap_weight * piece
    return running


def shrink(field, rim_in, rim_out):
    rows_done = shrink_axis(field, field.ndim - 2, rim_in, rim_out)
    return shrink_axis(rows_done, field.ndim - 1, rim_in, rim_out)


def grow_axis(field, along, rim_in, rim_out):
    length = field.shape[along]
    before = lax.slice_in_dim(field, 0, length - 2, 1, along)
    middle = lax.slice_in_dim(field, 1, length - 1, 1, along)
    behind = lax.slice_in_dim(field, 2, length, 1, along)
    at_even = (before + 6.0 * middle + behind) * 0.125
    at_odd = (middle + behind) * 0.5
    paired = jnp.stack([at_even, at_odd], axis=along + 1)
    new_shape = list(middle.shape)
    new_shape[along] = new_shape[along] * 2
    paired = paired.reshape(new_shape)
    excess = 2 * rim_in - 2 - rim_out
    return lax.slice_in_dim(paired, excess, new_shape[along] - excess, 1, along)


def grow(field, rim_in, rim_out):
    rows_done = grow_axis(field, field.ndim - 2, rim_in, rim_out)
    return grow_axis(rows_done, field.ndim - 1, rim_in, rim_out)


def pad_edges(field, depth):
    widths = [(0, 0)] * (field.ndim - 2) + [(depth, depth), (depth, depth)]
    return jnp.pad(field, widths)


def reference(scenes, cloud, destination, offset, counts):
    per_row = TS // BS
    blocks_all = N_TX * S_DEV
    living = (jnp.arange(S_DEV, dtype=jnp.int32)[None, None, :] < counts[:, :, None]).reshape(N_TY, blocks_all)
    coverage = cloud.astype(jnp.float32) * living[:, :, None].astype(jnp.float32)
    weighted = scenes.astype(jnp.float32) * coverage[:, :, None, :]
    top_row = destination * TS + (offset // per_row) * BS
    left_col = jnp.arange(N_TY, dtype=jnp.int32)[:, None] * TS + (offset % per_row) * BS
    offsets_in = jnp.arange(BS, dtype=jnp.int32)
    rows = top_row[:, :, None, None] + offsets_in[None, None, :, None]
    cols = left_col[:, :, None, None] + offsets_in[None, None, None, :]
    rows = jnp.broadcast_to(rows, (N_TY, blocks_all, BS, BS))
    cols = jnp.broadcast_to(cols, (N_TY, blocks_all, BS, BS))
    values = weighted.reshape(N_TY, blocks_all, BANDS, BS, BS).transpose(2, 0, 1, 3, 4)
    total = jnp.zeros((BANDS, NR, NC), jnp.float32).at[:, rows, cols].add(values)
    weight_sum = jnp.zeros((NR, NC), jnp.float32).at[rows, cols].add(coverage.reshape(N_TY, blocks_all, BS, BS))
    stacked = jnp.concatenate([total, weight_sum[None]], axis=0)
    pyramid = [stacked]
    for tier_index in range(1, LEVELS):
        pyramid.append(shrink(pad_edges(pyramid[-1], 2), 2, 0))
    summit = pyramid[-1]
    collapsed = summit[:BANDS] / (BACKGROUND + summit[BANDS])
    for tier_index in range(LEVELS - 2, -1, -1):
        current = pyramid[tier_index]
        coarser = pyramid[tier_index + 1]
        detail = current[:BANDS] - grow(pad_edges(coarser[:BANDS], 1), 1, 0)
        band_part = detail / (BACKGROUND + current[BANDS])
        collapsed = band_part + grow(pad_edges(collapsed, 1), 1, 0)
    blended = collapsed.astype(jnp.bfloat16)
    return blended.reshape(BANDS, NR, N_TY, TS).transpose(0, 2, 3, 1)
```

```python
import functools

import jax
import jax.numpy as jnp
import ml_dtypes
import numpy as np
from jax import lax
from jax.experimental import pallas as pl
from jax.experimental.pallas import tpu as pltpu
from jax.sharding import PartitionSpec as P

TS = 128
BS = 16
S_DEV = 64
SLOTS = 64
TAPS = (0.0625, 0.25, 0.375, 0.25, 0.0625)
BACKGROUND = 0.25
MESH = pl.DeviceIdType.MESH
BF = jnp.bfloat16
F32 = jnp.float32
REACH = {1: (-1, 64), 2: (-1, 33), 3: (-1, 17)}


def stack_order():
    left, right, rest = [], [], []
    for level, (first, last) in REACH.items():
        width = 2 * (2**level - 1)
        for p in range(first, last + 1):
            entry = (level, p)
            if 2**level * p - width < 0:
                left.append(entry)
            elif 2**level * p + width >= TS:
                right.append(entry)
            else:
                rest.append(entry)
    assert len(left) == 8 and len(right) == 8 and len(rest) <= 112
    return left + right + rest


def operators(is_first, is_last):
    order = stack_order()
    low, high = (0 if is_first else -TS), (TS if is_last else 2 * TS)
    down = {0: np.eye(3 * TS)}
    begin = {0: -TS}
    for p in range(3 * TS):
        if not low <= p - TS < high:
            down[0][p] = 0
    for level in (1, 2, 3):
        extent = 3 * TS >> level
        begin[level] = -(TS >> level)
        matrix = np.zeros((extent, 3 * TS))
        for i in range(extent):
            p = begin[level] + i
            if not (low >> level) <= p < (high >> level):
                continue
            for a, tap in enumerate(TAPS):
                source = 2 * p + a - 2 - begin[level - 1]
                if 0 <= source < down[level - 1].shape[0]:
                    matrix[i] += tap * down[level - 1][source]
        down[level] = matrix
    where = {entry: i for i, entry in enumerate(order)}
    d = np.zeros((TS, 3 * TS))
    for (level, p), i in where.items():
        d[i] = down[level][p - begin[level]]

    def grown(p):
        half = p // 2
        if p % 2 == 0:
            return ((half - 1, 0.125), (half, 0.75), (half + 1, 0.125))
        return ((half, 0.5), (half + 1, 0.5))

    up = np.zeros((TS, TS))
    for (level, p), i in where.items():
        if level < 3 and (low >> level) <= p < (high >> level):
            for q, weight in grown(p):
                up[i, where[(level + 1, q)]] += weight
    f = np.zeros((TS, TS))
    for p in range(TS):
        for q, weight in grown(p):
            f[p, where[(1, q)]] += weight
    q = f @ (np.eye(TS) + up + up @ up)
    return d, up, f, q


def bf16(x):
    return x.astype(ml_dtypes.bfloat16)


def tables():
    order = stack_order()
    levels = np.array([level for level, _ in order] + [0] * (TS - len(order)))
    same = ((levels[:, None] == levels[None, :]) & (levels[:, None] > 0)).astype(np.float32)
    dc, pc, qc, dr, pfr, qr = [], [], [], [], [], []
    for variant in range(4):
        d, up, f, q = operators(variant % 2 == 1, variant >= 2)
        mid = operators(False, False)[0]
        to_left = mid[8:16, 2 * TS :]
        to_right = mid[0:8, :TS]
        edges = np.concatenate([to_left, to_right])
        own = np.concatenate([d[:, TS : 2 * TS], edges])
        top = bf16(own).astype(np.float64)
        low = own - top
        three = np.concatenate([top, top, low], axis=1)
        assert np.all(bf16(low).astype(np.float64) == low)
        assert np.all(bf16(up).astype(np.float64) == up)
        q_top = bf16(q).astype(np.float64)
        q_three = np.concatenate([q_top, q_top, q - q_top], axis=1)
        dc.append(three)
        dr.append(three[:TS].T)
        pc.append(np.concatenate([up, up], axis=1))
        qc.append(q_three)
        pf = np.concatenate([up.T, f.T], axis=1)
        pfr.append(np.concatenate([pf, pf], axis=0))
        qr.append(q_three.T)
    de = dc[0][TS:]
    fc = np.concatenate([f, f], axis=1)
    return [bf16(np.stack(x)) for x in (dc, pc, qc, dr, pfr, qr)] + [bf16(de), bf16(fc), same]


def split(x, axis, three=False):
    top = x.astype(BF)
    low = (x - top.astype(F32)).astype(BF)
    return jnp.concatenate([top, low, top] if three else [top, low], axis=axis)


def dot(a, b):
    return jnp.dot(a, b, preferred_element_type=F32)


def regroup(x):
    row = lax.broadcasted_iota(jnp.int32, x.shape, 1)
    col = lax.broadcasted_iota(jnp.int32, x.shape, 2) // BS
    for d in (4, 2, 1):
        row_bit, col_bit = (row // d) % 2, (col // d) % 2
        ahead = pltpu.roll(pltpu.roll(x, 8 - d, 1), BS * d, 2)
        if d == 4:
            x = jnp.where(row_bit == col_bit, x, ahead)
        else:
            behind = pltpu.roll(pltpu.roll(x, d, 1), TS - BS * d, 2)
            x = jnp.where(row_bit == col_bit, x, jnp.where(row_bit == 0, ahead, behind))
    return x


def kernel(
    n_tx, n_ty, own, spread, rows, strip, strip_rows,
    scenes, cloud, destination, offset, counts, same,
    dc_h, pc_h, qc_h, dr_h, pfr_h, qr_h, de_h, fc_h,
    out,
    dc, pc, qc, dr, pfr, qr, de, fc,
    merged, sent, landed, code_out, code_in, field, cols_out, cols_in, rows_out, rows_in,
    final, staged, strip_out, strip_in,
    const_sem, block_send, block_recv, code_send, code_recv, halo_send, halo_recv, strip_send, strip_recv,
):
    me, col = lax.axis_index("tx"), lax.axis_index("ty")
    chans = own + 1
    variant_c = jnp.where(col == 0, 1, 0) + jnp.where(col == n_ty - 1, 2, 0)
    variant_r = jnp.where(me == 0, 1, 0) + jnp.where(me == n_tx - 1, 2, 0)

    barrier = pltpu.get_barrier_semaphore()
    for d in range(1, n_tx):
        pl.semaphore_signal(barrier, inc=1, device_id={"tx": lax.rem(me + d, n_tx)}, device_id_type=MESH)

    @pl.when(col > 0)
    def _():
        pl.semaphore_signal(barrier, inc=1, device_id={"ty": col - 1}, device_id_type=MESH)

    @pl.when(col < n_ty - 1)
    def _():
        pl.semaphore_signal(barrier, inc=1, device_id={"ty": col + 1}, device_id_type=MESH)

    loads = [
        pltpu.make_async_copy(src, dst, const_sem.at[i])
        for i, (src, dst) in enumerate(
            (
                (dc_h.at[variant_c], dc), (pc_h.at[variant_c], pc), (qc_h.at[variant_c], qc),
                (dr_h.at[variant_r], dr), (pfr_h.at[variant_r], pfr), (qr_h.at[variant_r], qr),
                (de_h, de), (fc_h, fc),
            )
        )
    ]
    for load in loads:
        load.start()

    dest = jnp.broadcast_to(destination[...], (S_DEV, S_DEV))
    dest_t = dest.T
    lane = lax.broadcasted_iota(jnp.int32, (S_DEV, S_DEV), 1)
    sub = lax.broadcasted_iota(jnp.int32, (S_DEV, S_DEV), 0)
    live = jnp.broadcast_to(counts[...], (S_DEV, S_DEV))
    earlier = (dest == dest_t) & (sub < lane)
    rank = jnp.sum(jnp.where(earlier, 1.0, 0.0), axis=0, keepdims=True)
    target = jnp.where(lane[:1] < live[:1], dest[:1].astype(F32) * spread + rank, -1.0)
    wide = lax.broadcasted_iota(jnp.int32, (S_DEV, 8 * S_DEV), 1)
    spread_out = jnp.where(wide // 8 == lax.broadcasted_iota(jnp.int32, wide.shape, 0), 1.0, 0.0).astype(BF)
    key = dot(jnp.broadcast_to(target, (16, S_DEV)).astype(BF), spread_out)[:1]
    key = jnp.where(key < 0, -1.0, key + 256.0 * (wide[:1] % 8).astype(F32))

    merged[...] = jnp.zeros_like(merged)
    for half in range(2):
        at = slice(half * TS, half * TS + TS)
        for b in range(own):
            merged[half, pl.ds(b, S_DEV, stride=8), :] = scenes[0, :, b, at].astype(F32)
        merged[half, pl.ds(own, S_DEV, stride=8), :] = cloud[0, :, at].astype(F32)
    everything = jnp.concatenate([merged[0], merged[1]], axis=1).astype(BF)
    line = lax.broadcasted_iota(jnp.int32, (rows, 1), 0)

    code_lanes = code_out.shape[2]
    lanes = lax.broadcasted_iota(jnp.int32, (S_DEV, code_lanes), 1)
    rank_t = jnp.broadcast_to(rank, (S_DEV, S_DEV)).T[:, :1]
    seat = jnp.where((lanes % spread).astype(F32) == rank_t, 1.0, 0.0).astype(BF)
    tall = lax.broadcasted_iota(jnp.int32, (max(16, n_tx), S_DEV), 0)
    across = lax.broadcasted_iota(jnp.int32, tall.shape, 1)
    marks = jnp.where((tall == destination[...]) & (across < counts[...]), (offset[...] + 1).astype(F32), 0.0)
    codes = dot(marks.astype(BF), seat) + 128.0 * (lanes[:1] // spread).astype(F32)
    for t in range(n_tx):
        code_out[t] = jnp.broadcast_to(codes[t : t + 1], (8, code_lanes))

    def pack(t):
        slot = t * spread + line % spread
        line_key = (256 * (line // spread) + slot).astype(F32)
        chooser = jnp.where(line_key == key, 1.0, 0.0).astype(BF)
        return dot(chooser, everything).astype(BF)

    pl.semaphore_wait(barrier, n_tx - 1 + jnp.where(col > 0, 1, 0) + jnp.where(col < n_ty - 1, 1, 0))

    def exchange(src, dst, send, recv, other):
        return pltpu.make_async_remote_copy(
            src_ref=src.at[other], dst_ref=dst.at[me], send_sem=send.at[other], recv_sem=recv.at[me],
            device_id={"tx": other}, device_id_type=MESH,
        )

    def incoming(src, dst, send, recv, other):
        return pltpu.make_async_remote_copy(
            src_ref=src.at[other], dst_ref=dst.at[other], send_sem=send.at[other], recv_sem=recv.at[other],
            device_id={"tx": other}, device_id_type=MESH,
        )

    peers = [lax.rem(me + d, n_tx) for d in range(1, n_tx)]
    for peer in peers:
        exchange(code_out, code_in, code_send, code_recv, peer).start()
        sent[peer] = pack(peer)
        exchange(sent, landed, block_send, block_recv, peer).start()

    row_code = lax.broadcasted_iota(jnp.int32, (chans * SLOTS, 1), 0)
    row_code = (128 * (row_code // SLOTS) + row_code % SLOTS + 1).astype(F32)
    here = lax.broadcasted_iota(jnp.int32, (rows, rows), 0)
    there = lax.broadcasted_iota(jnp.int32, (rows, rows), 1)
    cover_of = jnp.where(there == own * spread + here % spread, 1.0, 0.0).astype(BF)

    def place(block, code):
        values = block.astype(F32)
        if spread % 8 == 0:
            cover = values[own * spread :]
            product = jnp.concatenate([values[: own * spread] * jnp.concatenate([cover] * own), cover])
        else:
            cover = dot(cover_of, block)
            product = values * jnp.where(line >= own * spread, 1.0, cover)
        landing = jnp.where(row_code == code, 1.0, 0.0).astype(BF)
        top = product.astype(BF)
        low = (product - top.astype(F32)).astype(BF)
        return dot(landing, top) + dot(landing, low)

    total = place(pack(me), code_out[me][:1, :rows])
    for peer in peers:
        incoming(code_out, code_in, code_send, code_recv, peer).wait_recv()
        incoming(sent, landed, block_send, block_recv, peer).wait_recv()
        total += place(landed[peer], code_in[peer][:1, :rows])

    per_row = TS // BS
    for half in range(2):
        part = total[:, half * TS : half * TS + TS].reshape(chans * per_row, 8, TS)
        field[:, :, half] = regroup(part).reshape(chans, per_row, 8, TS)

    for load in loads:
        load.wait()

    tiles = []
    stack = []
    for c in range(chans):
        tile = field[c].reshape(TS, TS).T
        tiles.append(tile)
        got = dot(dc[...], split(tile, 0, three=True))
        stack.append(got[:TS])
        cols_out[0, c] = got[TS : TS + 8]
        cols_out[1, c] = got[TS + 8 : TS + 16]

    def halo(axis, src, dst, side, place_at, other):
        return pltpu.make_async_remote_copy(
            src_ref=src.at[side], dst_ref=dst.at[1 - side], send_sem=halo_send.at[place_at + side],
            recv_sem=halo_recv.at[place_at + 1 - side], device_id={axis: other}, device_id_type=MESH,
        )

    def swap(axis, at, n, src, dst, place_at):
        @pl.when(at > 0)
        def _():
            halo(axis, src, dst, 0, place_at, at - 1).start()

        @pl.when(at < n - 1)
        def _():
            halo(axis, src, dst, 1, place_at, at + 1).start()

        @pl.when(at == 0)
        def _():
            dst[0] = jnp.zeros_like(dst[0])

        @pl.when(at == n - 1)
        def _():
            dst[1] = jnp.zeros_like(dst[1])

    def swapped(axis, at, n, src, dst, place_at):
        @pl.when(at > 0)
        def _():
            halo(axis, src, dst, 0, place_at, at - 1).wait_send()
            halo(axis, src, dst, 1, place_at, at - 1).wait_recv()

        @pl.when(at < n - 1)
        def _():
            halo(axis, src, dst, 1, place_at, at + 1).wait_send()
            halo(axis, src, dst, 0, place_at, at + 1).wait_recv()

    swap("ty", col, n_ty, cols_out, cols_in, 0)
    swapped("ty", col, n_ty, cols_out, cols_in, 0)
    for c in range(chans):
        stack[c] = jnp.concatenate([stack[c][:8] + cols_in[0, c], stack[c][8:16] + cols_in[1, c], stack[c][16:]], axis=0)

    flat = split(jnp.concatenate(stack, axis=0), 1, three=True)
    edges = lax.dot_general(de[...], flat, (((1,), (1,)), ((), ())), preferred_element_type=F32)
    rows_out[0] = edges[:8]
    rows_out[1] = edges[8:]
    swap("tx", me, n_tx, rows_out, rows_in, 2)
    deep = dot(flat, dr[...])
    swapped("tx", me, n_tx, rows_out, rows_in, 2)
    rim = jnp.concatenate([rows_in[0], rows_in[1], jnp.zeros((TS - 16, chans * TS), F32)], axis=0)
    deep = deep + rim.T

    weight = deep[own * TS :]
    detail = split(dot(split(deep[: own * TS], 1), pfr[...]), 1)
    scale = same[...] / (BACKGROUND + weight)
    bands = []
    finer = []
    for b in range(own):
        at = slice(b * TS, b * TS + TS)
        both = jnp.concatenate([detail[at, : 2 * TS], detail[at, 2 * TS :]], axis=0)
        bands.append((deep[at] - dot(pc[...], both[:, :TS])) * scale)
        finer.append(dot(fc[...], both[:, TS:]))
    lifted = dot(split(jnp.concatenate(bands, axis=0), 1, three=True), qr[...])
    share = 1.0 / (BACKGROUND + tiles[own])
    for b in range(own):
        at = slice(b * TS, b * TS + TS)
        final[b] = (tiles[b] - finer[b]) * share + dot(qc[...], split(lifted[at], 0, three=True))

    def strip_of(t):
        for b in range(own):
            staged[b * strip : (b + 1) * strip, :] = final[b, pl.ds(t * strip, strip), :]
        return staged[...].astype(BF)

    staged[...] = jnp.zeros_like(staged)
    for peer in peers:
        strip_out[peer] = strip_of(peer)
        exchange(strip_out, strip_in, strip_send, strip_recv, peer).start()
    strip_in[me] = strip_of(me)
    for peer in peers:
        incoming(strip_out, strip_in, strip_send, strip_recv, peer).wait_recv()
    for s in range(n_tx):
        got = strip_in[s].astype(F32)
        for b in range(own):
            out[b, 0, :, s * TS : (s + 1) * TS] = got[b * strip : (b + 1) * strip].astype(BF)
    for peer in peers:
        exchange(code_out, code_in, code_send, code_recv, peer).wait_send()
        exchange(sent, landed, block_send, block_recv, peer).wait_send()
        exchange(strip_out, strip_in, strip_send, strip_recv, peer).wait_send()


def solution(mesh):
    n_tx, n_ty = mesh.shape["tx"], mesh.shape["ty"]
    consts = tables()

    def local(scenes, cloud, destination, offset, counts):
        own = scenes.shape[2]
        chans = own + 1
        spread = max(2, 2 * S_DEV // n_tx)
        rows = -(-chans * spread // 16) * 16
        code_lanes = -(-rows // TS) * TS
        strip = TS // n_tx
        strip_rows = -(-own * strip // 16) * 16
        moved = consts[:6]
        fixed = consts[6:8]
        vmem = pl.BlockSpec(memory_space=pltpu.VMEM)
        return pl.pallas_call(
            functools.partial(kernel, n_tx, n_ty, own, spread, rows, strip, strip_rows),
            out_shape=jax.ShapeDtypeStruct((own, 1, strip, TS * n_tx), BF),
            in_specs=[vmem] * 6 + [pl.BlockSpec(memory_space=pl.ANY)] * 8,
            out_specs=vmem,
            scratch_shapes=[pltpu.VMEM(x.shape[1:], BF) for x in moved]
            + [pltpu.VMEM(x.shape, BF) for x in fixed]
            + [
                pltpu.VMEM((2, 8 * S_DEV, TS), F32),
                pltpu.VMEM((n_tx, rows, BS * BS), BF),
                pltpu.VMEM((n_tx, rows, BS * BS), BF),
                pltpu.VMEM((n_tx, 8, code_lanes), F32),
                pltpu.VMEM((n_tx, 8, code_lanes), F32),
                pltpu.VMEM((chans, TS // BS, 2, 8, TS), F32),
                pltpu.VMEM((2, chans, 8, TS), F32),
                pltpu.VMEM((2, chans, 8, TS), F32),
                pltpu.VMEM((2, 8, chans * TS), F32),
                pltpu.VMEM((2, 8, chans * TS), F32),
                pltpu.VMEM((own, TS, TS), F32),
                pltpu.VMEM((strip_rows, TS), F32),
                pltpu.VMEM((n_tx, strip_rows, TS), BF),
                pltpu.VMEM((n_tx, strip_rows, TS), BF),
                pltpu.SemaphoreType.DMA((8,)),
            ]
            + [pltpu.SemaphoreType.DMA((n_tx,))] * 4
            + [pltpu.SemaphoreType.DMA((4,))] * 2
            + [pltpu.SemaphoreType.DMA((n_tx,))] * 2,
            compiler_params=pltpu.CompilerParams(
                collective_id=0, has_side_effects=True, vmem_limit_bytes=48 * 1024 * 1024
            ),
        )(scenes, cloud, destination, offset, counts, jnp.asarray(consts[8]), *(jnp.asarray(x) for x in moved + fixed))

    placed = (
        P(("region", "ty"), "tx", "band", None),
        P(("region", "ty"), "tx", None),
        P(("region", "ty"), "tx"),
        P(("region", "ty"), "tx"),
        P(("region", "ty"), "tx"),
    )
    return jax.shard_map(
        local, mesh=mesh, in_specs=placed, out_specs=P("band", ("region", "ty"), "tx", None), check_vma=False
    )
```

```python
import functools

import jax
import jax.numpy as jnp
import ml_dtypes
import numpy as np
from jax import lax
from jax.experimental import pallas as pl
from jax.experimental.pallas import tpu as pltpu
from jax.sharding import PartitionSpec as P

TS = 128
BS = 16
S_DEV = 64
SLOTS = 64
TAPS = (0.0625, 0.25, 0.375, 0.25, 0.0625)
BACKGROUND = 0.25
MESH = pl.DeviceIdType.MESH
BF = jnp.bfloat16
F32 = jnp.float32
REACH = {1: (-1, 64), 2: (-1, 33), 3: (-1, 17)}


def stack_order():
    left, right, rest = [], [], []
    for level, (first, last) in REACH.items():
        width = 2 * (2**level - 1)
        for p in range(first, last + 1):
            entry = (level, p)
            if 2**level * p - width < 0:
                left.append(entry)
            elif 2**level * p + width >= TS:
                right.append(entry)
            else:
                rest.append(entry)
    assert len(left) == 8 and len(right) == 8 and len(rest) <= 112
    return left + right + rest


def operators(is_first, is_last):
    order = stack_order()
    low, high = (0 if is_first else -TS), (TS if is_last else 2 * TS)
    down = {0: np.eye(3 * TS)}
    begin = {0: -TS}
    for p in range(3 * TS):
        if not low <= p - TS < high:
            down[0][p] = 0
    for level in (1, 2, 3):
        extent = 3 * TS >> level
        begin[level] = -(TS >> level)
        matrix = np.zeros((extent, 3 * TS))
        for i in range(extent):
            p = begin[level] + i
            if not (low >> level) <= p < (high >> level):
                continue
            for a, tap in enumerate(TAPS):
                source = 2 * p + a - 2 - begin[level - 1]
                if 0 <= source < down[level - 1].shape[0]:
                    matrix[i] += tap * down[level - 1][source]
        down[level] = matrix
    where = {entry: i for i, entry in enumerate(order)}
    d = np.zeros((TS, 3 * TS))
    for (level, p), i in where.items():
        d[i] = down[level][p - begin[level]]

    def grown(p):
        half = p // 2
        if p % 2 == 0:
            return ((half - 1, 0.125), (half, 0.75), (half + 1, 0.125))
        return ((half, 0.5), (half + 1, 0.5))

    up = np.zeros((TS, TS))
    for (level, p), i in where.items():
        if level < 3 and (low >> level) <= p < (high >> level):
            for q, weight in grown(p):
                up[i, where[(level + 1, q)]] += weight
    f = np.zeros((TS, TS))
    for p in range(TS):
        for q, weight in grown(p):
            f[p, where[(1, q)]] += weight
    q = f @ (np.eye(TS) + up + up @ up)
    return d, up, f, q


def bf16(x):
    return x.astype(ml_dtypes.bfloat16)


def tables():
    order = stack_order()
    levels = np.array([level for level, _ in order] + [0] * (TS - len(order)))
    same = ((levels[:, None] == levels[None, :]) & (levels[:, None] > 0)).astype(np.float32)
    dc, pc, qc, dr, pfr, qr = [], [], [], [], [], []
    for variant in range(4):
        d, up, f, q = operators(variant % 2 == 1, variant >= 2)
        mid = operators(False, False)[0]
        to_left = mid[8:16, 2 * TS :]
        to_right = mid[0:8, :TS]
        edges = np.concatenate([to_left, to_right])
        own = np.concatenate([d[:, TS : 2 * TS], edges])
        top = bf16(own).astype(np.float64)
        low = own - top
        three = np.concatenate([top, top, low], axis=1)
        assert np.all(bf16(low).astype(np.float64) == low)
        assert np.all(bf16(up).astype(np.float64) == up)
        q_top = bf16(q).astype(np.float64)
        q_three = np.concatenate([q_top, q_top, q - q_top], axis=1)
        dc.append(three)
        dr.append(three[:TS].T)
        pc.append(np.concatenate([up, up], axis=1))
        qc.append(q_three)
        pf = np.concatenate([up.T, f.T], axis=1)
        pfr.append(np.concatenate([pf, pf], axis=0))
        qr.append(q_three.T)
    de = dc[0][TS:]
    fc = np.concatenate([f, f], axis=1)
    return [bf16(np.stack(x)) for x in (dc, pc, qc, dr, pfr, qr)] + [bf16(de), bf16(fc), same]


def split(x, axis, three=False):
    top = x.astype(BF)
    low = (x - top.astype(F32)).astype(BF)
    return jnp.concatenate([top, low, top] if three else [top, low], axis=axis)


def dot(a, b):
    return jnp.dot(a, b, preferred_element_type=F32)


def regroup(x):
    row = lax.broadcasted_iota(jnp.int32, x.shape, 1)
    col = lax.broadcasted_iota(jnp.int32, x.shape, 2) // BS
    for d in (4, 2, 1):
        row_bit, col_bit = (row // d) % 2, (col // d) % 2
        ahead = pltpu.roll(pltpu.roll(x, 8 - d, 1), BS * d, 2)
        if d == 4:
            x = jnp.where(row_bit == col_bit, x, ahead)
        else:
            behind = pltpu.roll(pltpu.roll(x, d, 1), TS - BS * d, 2)
            x = jnp.where(row_bit == col_bit, x, jnp.where(row_bit == 0, ahead, behind))
    return x


def kernel(
    n_tx, n_ty, own, groups, spread, seats, strip,
    destination, offset, counts, scenes_h, cloud_h, *refs,
):
    consts_h, refs = refs[:9], refs[9:]
    out, refs = refs[0], refs[1:]
    consts, refs = refs[:9], refs[9:]
    dc, pc, qc, dr, pfr, qr, de, fc, same = consts
    (scenes, cloud, sent, landed, code_out, code_in, field, tiles, stack, deep, cols_out, cols_in, rows_out, rows_in,
     ratio, final, staged, strip_out, strip_in,
     const_sem, in_sem, block_send, block_recv, code_send, code_recv, halo_send, halo_recv, strip_send, strip_recv) = refs
    me, col = lax.axis_index("tx"), lax.axis_index("ty")
    chans = own + 1
    pixels = BS * BS
    variant_c = jnp.where(col == 0, 1, 0) + jnp.where(col == n_ty - 1, 2, 0)
    variant_r = jnp.where(me == 0, 1, 0) + jnp.where(me == n_tx - 1, 2, 0)
    fetch = [
        pltpu.make_async_copy(scenes_h.at[0], scenes, in_sem.at[0]),
        pltpu.make_async_copy(cloud_h.at[0], cloud, in_sem.at[1]),
    ]
    for f in fetch:
        f.start()

    barrier = pltpu.get_barrier_semaphore()
    for d in range(1, n_tx):
        pl.semaphore_signal(barrier, inc=1, device_id={"tx": lax.rem(me + d, n_tx)}, device_id_type=MESH)

    @pl.when(col > 0)
    def _():
        pl.semaphore_signal(barrier, inc=1, device_id={"ty": col - 1}, device_id_type=MESH)

    @pl.when(col < n_ty - 1)
    def _():
        pl.semaphore_signal(barrier, inc=1, device_id={"ty": col + 1}, device_id_type=MESH)

    variants = [variant_c] * 3 + [variant_r] * 3 + [None] * 3
    loads = [
        pltpu.make_async_copy(src if v is None else src.at[v], dst, const_sem.at[i])
        for i, (src, dst, v) in enumerate(zip(consts_h, consts, variants))
    ]
    for load in loads:
        load.start()

    dest = jnp.broadcast_to(destination[...], (S_DEV, S_DEV))
    lane = lax.broadcasted_iota(jnp.int32, (S_DEV, S_DEV), 1)
    sub = lax.broadcasted_iota(jnp.int32, (S_DEV, S_DEV), 0)
    live = jnp.broadcast_to(counts[...], (S_DEV, S_DEV))
    earlier = (dest == dest.T) & (sub < lane)
    rank = jnp.sum(jnp.where(earlier, 1.0, 0.0), axis=0, keepdims=True)
    target = jnp.where(lane[:1] < live[:1], dest[:1].astype(F32) * seats + rank, -1.0)
    seat_id = lax.broadcasted_iota(jnp.int32, (n_tx * seats, 1), 0).astype(F32)
    chooser = jnp.where(seat_id == target, 1.0, 0.0).astype(BF)

    lanes = lax.broadcasted_iota(jnp.int32, (S_DEV, TS), 1)
    rank_t = jnp.broadcast_to(rank, (S_DEV, S_DEV)).T[:, :1]
    seat = jnp.where(lanes.astype(F32) == rank_t, 1.0, 0.0).astype(BF)
    tall = lax.broadcasted_iota(jnp.int32, (max(16, n_tx), S_DEV), 0)
    across = lax.broadcasted_iota(jnp.int32, tall.shape, 1)
    marks = jnp.where((tall == destination[...]) & (across < counts[...]), (offset[...] + 1).astype(F32), 0.0)
    codes = dot(marks.astype(BF), seat)
    for t in range(n_tx):
        code_out[t] = jnp.broadcast_to(codes[t : t + 1], (8, TS))
    code_in[me] = code_out[me]

    def pack(first, last):
        for c in range(first, last):
            got = dot(chooser, cloud[...] if c == 0 else scenes[c - 1]).astype(BF)
            sent[:, c] = got.reshape(n_tx, seats, pixels)

    for f in reversed(fetch):
        f.wait()
    each = own // groups
    spans = [(0 if g == 0 else 1 + g * each, 1 + (g + 1) * each) for g in range(groups)]
    pack(*spans[0])
    pl.semaphore_wait(barrier, n_tx - 1 + jnp.where(col > 0, 1, 0) + jnp.where(col < n_ty - 1, 1, 0))

    def exchange(src, dst, send, recv, other, g=None, span=None, slot=None):
        slot = me if slot is None else slot
        if span is not None:
            src, dst = src.at[other, span[0] : span[1]], dst.at[slot, span[0] : span[1]]
            send, recv = send.at[g, other], recv.at[g, slot]
        elif g is not None:
            src, dst, send, recv = src.at[g, other], dst.at[g, slot], send.at[g, other], recv.at[g, slot]
        else:
            src, dst, send, recv = src.at[other], dst.at[slot], send.at[other], recv.at[slot]
        return pltpu.make_async_remote_copy(
            src_ref=src, dst_ref=dst, send_sem=send, recv_sem=recv, device_id={"tx": other}, device_id_type=MESH
        )

    peers = [lax.rem(me + d, n_tx) for d in range(1, n_tx)]
    code_refs = (code_out, code_in, code_send, code_recv)
    block_refs = (sent, landed, block_send, block_recv)
    strip_refs = (strip_out, strip_in, strip_send, strip_recv)
    for peer in peers:
        exchange(*code_refs, peer).start()
    for g, span in enumerate(spans):
        if g:
            pack(*span)
        for peer in peers:
            exchange(*block_refs, peer, g, span).start()
        landed[me, span[0] : span[1]] = sent[me, span[0] : span[1]]

    def halo(axis, src, dst, side, g, place_at, other, sending):
        span = slice(*spans[g])
        return pltpu.make_async_remote_copy(
            src_ref=src.at[side, span], dst_ref=dst.at[1 - side, span], send_sem=halo_send.at[g, place_at + side],
            recv_sem=halo_recv.at[g, place_at + 1 - side], device_id={axis: other}, device_id_type=MESH,
        )

    def swap(axis, at, n, src, dst, g, place_at):
        span = slice(*spans[g])

        @pl.when(at > 0)
        def _():
            halo(axis, src, dst, 0, g, place_at, at - 1, True).start()

        @pl.when(at < n - 1)
        def _():
            halo(axis, src, dst, 1, g, place_at, at + 1, True).start()

        @pl.when(at == 0)
        def _():
            dst[0, span] = jnp.zeros_like(dst[0, span])

        @pl.when(at == n - 1)
        def _():
            dst[1, span] = jnp.zeros_like(dst[1, span])

    def swapped(axis, at, n, src, dst, g, place_at):
        @pl.when(at > 0)
        def _():
            halo(axis, src, dst, 0, g, place_at, at - 1, True).wait_send()
            halo(axis, src, dst, 1, g, place_at, at - 1, False).wait_recv()

        @pl.when(at < n - 1)
        def _():
            halo(axis, src, dst, 1, g, place_at, at + 1, True).wait_send()
            halo(axis, src, dst, 0, g, place_at, at + 1, False).wait_recv()

    cols = ("ty", col, n_ty, cols_out, cols_in)
    line = ("tx", me, n_tx, rows_out, rows_in)
    landing = []

    def stage_a(g):
        first, last = spans[g]
        if g == 0:
            for peer in peers:
                exchange(*code_refs, peer, slot=peer).wait_recv()
            slot_id = lax.broadcasted_iota(jnp.int32, (SLOTS, 1), 0).astype(F32) + 1.0
            found = [jnp.where(slot_id == code_in[s][:1, :seats], 1.0, 0.0) for s in range(n_tx)]
            landing.append(jnp.concatenate(found * 2, axis=1).astype(BF))
        for peer in peers:
            exchange(*block_refs, peer, g, spans[g], slot=peer).wait_recv()
        cover = jnp.concatenate([landed[s, 0] for s in range(n_tx)], axis=0)
        wide = cover.astype(F32)
        for c in range(first, last):
            if c == 0:
                total = dot(landing[0][:, : n_tx * seats], cover)
            else:
                values = jnp.concatenate([landed[s, c] for s in range(n_tx)], axis=0).astype(F32)
                total = dot(landing[0], split(values * wide, 0))
            for half in range(2):
                part = total[:, half * TS : half * TS + TS].reshape(TS // BS, 8, TS)
                field[c, :, half] = regroup(part)
        for c in range(first, last):
            tile = field[c].reshape(TS, TS).T
            tiles[c] = tile
            if c == 0:
                for i in (0, 3, 6, 1, 2, 4, 5, 7, 8):
                    loads[i].wait()
            got = dot(dc[...], split(tile, 0, three=True))
            stack[c] = got[:TS]
            cols_out[0, c] = got[TS : TS + 8]
            cols_out[1, c] = got[TS + 8 : TS + 16]
        swap(*cols, g, 0)

    def stage_b(g):
        first, last = spans[g]
        swapped(*cols, g, 0)
        parts = []
        for c in range(first, last):
            whole = stack[c]
            parts += [whole[:8] + cols_in[0, c], whole[8:16] + cols_in[1, c], whole[16:]]
        flat = split(jnp.concatenate(parts, axis=0), 1, three=True)
        edges = lax.dot_general(de[...], flat, (((1,), (1,)), ((), ())), preferred_element_type=F32)
        for c in range(first, last):
            at = slice((c - first) * TS, (c - first + 1) * TS)
            rows_out[0, c] = edges[:8, at]
            rows_out[1, c] = edges[8:, at]
        swap(*line, g, 2)
        got = dot(flat, dr[...])
        for c in range(first, last):
            deep[c] = got[(c - first) * TS : (c - first + 1) * TS]

    def stage_c(g):
        first, last = spans[g]
        swapped(*line, g, 2)
        for c in range(first, last):
            rim = jnp.concatenate([rows_in[0, c], rows_in[1, c], jnp.zeros((TS - 16, TS), F32)], axis=0)
            deep[c] = deep[c] + rim.T
        if g == 0:
            ratio[0] = same[...] / (BACKGROUND + deep[0])
            ratio[1] = 1.0 / (BACKGROUND + tiles[0])
        mine = range(max(first, 1), last)
        whole = jnp.concatenate([deep[c] for c in mine], axis=0)
        detail = split(dot(split(whole, 1), pfr[...]), 1)
        bands = []
        finer = []
        for i, c in enumerate(mine):
            at = slice(i * TS, i * TS + TS)
            both = jnp.concatenate([detail[at, : 2 * TS], detail[at, 2 * TS :]], axis=0)
            bands.append((deep[c] - dot(pc[...], both[:, :TS])) * ratio[0])
            finer.append(dot(fc[...], both[:, TS:]))
        lifted = dot(split(jnp.concatenate(bands, axis=0), 1, three=True), qr[...])
        for i, c in enumerate(mine):
            at = slice(i * TS, i * TS + TS)
            final[i] = (tiles[c] - finer[i]) * ratio[1] + dot(qc[...], split(lifted[at], 0, three=True))
        for peer in peers:
            strip_out[g, peer] = strip_of(peer)
            exchange(*strip_refs, peer, g).start()
        strip_in[g, me] = strip_of(me)

    staged[...] = jnp.zeros_like(staged)

    def strip_of(t):
        for i in range(each):
            staged[i * strip : (i + 1) * strip, :] = final[i, pl.ds(t * strip, strip), :]
        return staged[...].astype(BF)

    for step in range(groups + 1):
        if step < groups:
            stage_a(step)
        if step > 0:
            stage_c(step - 1)
        if step < groups:
            stage_b(step)
    for g in range(groups):
        for peer in peers:
            exchange(*strip_refs, peer, g, slot=peer).wait_recv()
        for s in range(n_tx):
            got = strip_in[g, s].astype(F32)
            for i in range(each):
                out[g * each + i, 0, :, s * TS : (s + 1) * TS] = got[i * strip : (i + 1) * strip].astype(BF)
    for peer in peers:
        exchange(*code_refs, peer).wait_send()
        for g in range(groups):
            exchange(*block_refs, peer, g, spans[g]).wait_send()
            exchange(*strip_refs, peer, g).wait_send()


def solution(mesh):
    n_tx, n_ty = mesh.shape["tx"], mesh.shape["ty"]
    consts = tables()

    def local(scenes, cloud, destination, offset, counts):
        own = scenes.shape[2]
        chans = own + 1
        groups = 3 if own % 3 == 0 else 1
        each = own // groups
        spread = max(2, 2 * S_DEV // n_tx)
        seats = -(-spread // 16) * 16
        strip = TS // n_tx
        strip_rows = -(-each * strip // 16) * 16
        pixels = BS * BS
        vmem = pl.BlockSpec(memory_space=pltpu.VMEM)
        hbm = pl.BlockSpec(memory_space=pltpu.HBM)
        dma = pltpu.SemaphoreType.DMA
        return pl.pallas_call(
            functools.partial(kernel, n_tx, n_ty, own, groups, spread, seats, strip),
            out_shape=jax.ShapeDtypeStruct((own, 1, strip, TS * n_tx), BF),
            in_specs=[vmem] * 3 + [hbm] * 11,
            out_specs=vmem,
            scratch_shapes=[pltpu.VMEM(x.shape[1:], BF) for x in consts[:6]]
            + [pltpu.VMEM(x.shape, BF) for x in consts[6:8]]
            + [
                pltpu.VMEM((TS, TS), F32),
                pltpu.VMEM((own, S_DEV, pixels), BF),
                pltpu.VMEM((S_DEV, pixels), BF),
                pltpu.VMEM((n_tx, chans, seats, pixels), BF),
                pltpu.VMEM((n_tx, chans, seats, pixels), BF),
                pltpu.VMEM((n_tx, 8, TS), F32),
                pltpu.VMEM((n_tx, 8, TS), F32),
                pltpu.VMEM((chans, TS // BS, 2, 8, TS), F32),
                pltpu.VMEM((chans, TS, TS), F32),
                pltpu.VMEM((chans, TS, TS), F32),
                pltpu.VMEM((chans, TS, TS), F32),
                pltpu.VMEM((2, chans, 8, TS), F32),
                pltpu.VMEM((2, chans, 8, TS), F32),
                pltpu.VMEM((2, chans, 8, TS), F32),
                pltpu.VMEM((2, chans, 8, TS), F32),
                pltpu.VMEM((2, TS, TS), F32),
                pltpu.VMEM((each, TS, TS), F32),
                pltpu.VMEM((strip_rows, TS), F32),
                pltpu.VMEM((groups, n_tx, strip_rows, TS), BF),
                pltpu.VMEM((groups, n_tx, strip_rows, TS), BF),
                dma((9,)), dma((2,)),
                dma((groups, n_tx)), dma((groups, n_tx)), dma((n_tx,)), dma((n_tx,)),
                dma((groups, 4)), dma((groups, 4)), dma((groups, n_tx)), dma((groups, n_tx)),
            ],
            compiler_params=pltpu.CompilerParams(
                collective_id=0, has_side_effects=True, vmem_limit_bytes=62 * 1024 * 1024
            ),
        )(destination, offset, counts, jnp.swapaxes(scenes, 1, 2), cloud, *(jnp.asarray(x) for x in consts))

    placed = (
        P(("region", "ty"), "tx", "band", None),
        P(("region", "ty"), "tx", None),
        P(("region", "ty"), "tx"),
        P(("region", "ty"), "tx"),
        P(("region", "ty"), "tx"),
    )
    return jax.shard_map(
        local, mesh=mesh, in_specs=placed, out_specs=P("band", ("region", "ty"), "tx", None), check_vma=False
    )
```

```python
import functools

import jax
import jax.numpy as jnp
import ml_dtypes
import numpy as np
from jax import lax
from jax.experimental import pallas as pl
from jax.experimental.pallas import tpu as pltpu
from jax.sharding import PartitionSpec as P

TS = 128
BS = 16
S_DEV = 64
SLOTS = 64
TAPS = (0.0625, 0.25, 0.375, 0.25, 0.0625)
BACKGROUND = 0.25
MESH = pl.DeviceIdType.MESH
BF = jnp.bfloat16
F32 = jnp.float32
REACH = {1: (-1, 64), 2: (-1, 33), 3: (-1, 17)}


def stack_order():
    left, right, rest = [], [], []
    for level, (first, last) in REACH.items():
        width = 2 * (2**level - 1)
        for p in range(first, last + 1):
            entry = (level, p)
            if 2**level * p - width < 0:
                left.append(entry)
            elif 2**level * p + width >= TS:
                right.append(entry)
            else:
                rest.append(entry)
    assert len(left) == 8 and len(right) == 8 and len(rest) <= 112
    return left + right + rest


def operators(is_first, is_last):
    order = stack_order()
    low, high = (0 if is_first else -TS), (TS if is_last else 2 * TS)
    down = {0: np.eye(3 * TS)}
    begin = {0: -TS}
    for p in range(3 * TS):
        if not low <= p - TS < high:
            down[0][p] = 0
    for level in (1, 2, 3):
        extent = 3 * TS >> level
        begin[level] = -(TS >> level)
        matrix = np.zeros((extent, 3 * TS))
        for i in range(extent):
            p = begin[level] + i
            if not (low >> level) <= p < (high >> level):
                continue
            for a, tap in enumerate(TAPS):
                source = 2 * p + a - 2 - begin[level - 1]
                if 0 <= source < down[level - 1].shape[0]:
                    matrix[i] += tap * down[level - 1][source]
        down[level] = matrix
    where = {entry: i for i, entry in enumerate(order)}
    d = np.zeros((TS, 3 * TS))
    for (level, p), i in where.items():
        d[i] = down[level][p - begin[level]]

    def grown(p):
        half = p // 2
        if p % 2 == 0:
            return ((half - 1, 0.125), (half, 0.75), (half + 1, 0.125))
        return ((half, 0.5), (half + 1, 0.5))

    up = np.zeros((TS, TS))
    for (level, p), i in where.items():
        if level < 3 and (low >> level) <= p < (high >> level):
            for q, weight in grown(p):
                up[i, where[(level + 1, q)]] += weight
    f = np.zeros((TS, TS))
    for p in range(TS):
        for q, weight in grown(p):
            f[p, where[(1, q)]] += weight
    q = f @ (np.eye(TS) + up + up @ up)
    return d, up, f, q


def bf16(x):
    return x.astype(ml_dtypes.bfloat16)


def tables():
    order = stack_order()
    levels = np.array([level for level, _ in order] + [0] * (TS - len(order)))
    same = ((levels[:, None] == levels[None, :]) & (levels[:, None] > 0)).astype(np.float32)
    dc, pc, qc, dr, pfr, qr = [], [], [], [], [], []
    for variant in range(4):
        d, up, f, q = operators(variant % 2 == 1, variant >= 2)
        mid = operators(False, False)[0]
        to_left = mid[8:16, 2 * TS :]
        to_right = mid[0:8, :TS]
        edges = np.concatenate([to_left, to_right])
        own = np.concatenate([d[:, TS : 2 * TS], edges])
        top = bf16(own).astype(np.float64)
        low = own - top
        three = np.concatenate([top, top, low], axis=1)
        assert np.all(bf16(low).astype(np.float64) == low)
        assert np.all(bf16(up).astype(np.float64) == up)
        q_top = bf16(q).astype(np.float64)
        q_three = np.concatenate([q_top, q_top, q - q_top], axis=1)
        dc.append(three)
        dr.append(three[:TS].T)
        pc.append(np.concatenate([up, up], axis=1))
        qc.append(q_three)
        pf = np.concatenate([up.T, f.T], axis=1)
        pfr.append(np.concatenate([pf, pf], axis=0))
        qr.append(q_three.T)
    de = dc[0][TS:]
    fc = np.concatenate([f, f], axis=1)
    return [bf16(np.stack(x)) for x in (dc, pc, qc, dr, pfr, qr)] + [bf16(de), bf16(fc), same]


def split(x, axis, three=False):
    top = x.astype(BF)
    low = (x - top.astype(F32)).astype(BF)
    return jnp.concatenate([top, low, top] if three else [top, low], axis=axis)


def dot(a, b):
    return jnp.dot(a, b, preferred_element_type=F32)


def regroup(x):
    row = lax.broadcasted_iota(jnp.int32, x.shape, 1)
    col = lax.broadcasted_iota(jnp.int32, x.shape, 2) // BS
    for d in (4, 2, 1):
        row_bit, col_bit = (row // d) % 2, (col // d) % 2
        ahead = pltpu.roll(pltpu.roll(x, 8 - d, 1), BS * d, 2)
        if d == 4:
            x = jnp.where(row_bit == col_bit, x, ahead)
        else:
            behind = pltpu.roll(pltpu.roll(x, d, 1), TS - BS * d, 2)
            x = jnp.where(row_bit == col_bit, x, jnp.where(row_bit == 0, ahead, behind))
    return x


def kernel(
    n_tx, n_ty, own, groups, spread, seats, strip,
    destination, offset, counts, scenes_h, cloud_h, *refs,
):
    consts_h, refs = refs[:9], refs[9:]
    out, refs = refs[0], refs[1:]
    consts, refs = refs[:9], refs[9:]
    dc, pc, qc, dr, pfr, qr, de, fc, same = consts
    (scenes, cloud, sent, landed, code_out, code_in, field, tiles, stack, deep, cols_out, cols_in, rows_out, rows_in,
     ratio, final, staged, strip_out, strip_in,
     const_sem, in_sem, block_send, block_recv, code_send, code_recv, halo_send, halo_recv, strip_send, strip_recv) = refs
    me, col = lax.axis_index("tx"), lax.axis_index("ty")
    chans = own + 1
    pixels = BS * BS
    variant_c = jnp.where(col == 0, 1, 0) + jnp.where(col == n_ty - 1, 2, 0)
    variant_r = jnp.where(me == 0, 1, 0) + jnp.where(me == n_tx - 1, 2, 0)
    fetch = [
        pltpu.make_async_copy(scenes_h.at[0], scenes, in_sem.at[0]),
        pltpu.make_async_copy(cloud_h.at[0], cloud, in_sem.at[1]),
    ]
    for f in fetch:
        f.start()

    barrier = pltpu.get_barrier_semaphore()
    for d in range(1, n_tx):
        pl.semaphore_signal(barrier, inc=1, device_id={"tx": lax.rem(me + d, n_tx)}, device_id_type=MESH)

    @pl.when(col > 0)
    def _():
        pl.semaphore_signal(barrier, inc=1, device_id={"ty": col - 1}, device_id_type=MESH)

    @pl.when(col < n_ty - 1)
    def _():
        pl.semaphore_signal(barrier, inc=1, device_id={"ty": col + 1}, device_id_type=MESH)

    variants = [variant_c] * 3 + [variant_r] * 3 + [None] * 3
    loads = [
        pltpu.make_async_copy(src if v is None else src.at[v], dst, const_sem.at[i])
        for i, (src, dst, v) in enumerate(zip(consts_h, consts, variants))
    ]
    for load in loads:
        load.start()

    dest = jnp.broadcast_to(destination[...], (S_DEV, S_DEV))
    lane = lax.broadcasted_iota(jnp.int32, (S_DEV, S_DEV), 1)
    sub = lax.broadcasted_iota(jnp.int32, (S_DEV, S_DEV), 0)
    live = jnp.broadcast_to(counts[...], (S_DEV, S_DEV))
    earlier = (dest == dest.T) & (sub < lane)
    rank = jnp.sum(jnp.where(earlier, 1.0, 0.0), axis=0, keepdims=True)
    target = jnp.where(lane[:1] < live[:1], dest[:1].astype(F32) * seats + rank, -1.0)
    seat_id = lax.broadcasted_iota(jnp.int32, (n_tx * seats, 1), 0).astype(F32)
    chooser = jnp.where(seat_id == target, 1.0, 0.0).astype(BF)

    lanes = lax.broadcasted_iota(jnp.int32, (S_DEV, TS), 1)
    rank_t = jnp.broadcast_to(rank, (S_DEV, S_DEV)).T[:, :1]
    seat = jnp.where(lanes.astype(F32) == rank_t, 1.0, 0.0).astype(BF)
    tall = lax.broadcasted_iota(jnp.int32, (max(16, n_tx), S_DEV), 0)
    across = lax.broadcasted_iota(jnp.int32, tall.shape, 1)
    marks = jnp.where((tall == destination[...]) & (across < counts[...]), (offset[...] + 1).astype(F32), 0.0)
    codes = dot(marks.astype(BF), seat)
    for t in range(n_tx):
        code_out[t] = jnp.broadcast_to(codes[t : t + 1], (8, TS))
    code_in[me] = code_out[me]

    def pack(first, last):
        for c in range(first, last):
            got = dot(chooser, cloud[...] if c == 0 else scenes[c - 1]).astype(BF)
            sent[:, c] = got.reshape(n_tx, seats, pixels)

    for f in reversed(fetch):
        f.wait()
    each = own // groups
    spans = [(0 if g == 0 else 1 + g * each, 1 + (g + 1) * each) for g in range(groups)]
    pack(*spans[0])
    pl.semaphore_wait(barrier, n_tx - 1 + jnp.where(col > 0, 1, 0) + jnp.where(col < n_ty - 1, 1, 0))

    def exchange(src, dst, send, recv, other, g=None, span=None, slot=None):
        slot = me if slot is None else slot
        if span is not None:
            src, dst = src.at[other, span[0] : span[1]], dst.at[slot, span[0] : span[1]]
            send, recv = send.at[g, other], recv.at[g, slot]
        elif g is not None:
            src, dst, send, recv = src.at[g, other], dst.at[g, slot], send.at[g, other], recv.at[g, slot]
        else:
            src, dst, send, recv = src.at[other], dst.at[slot], send.at[other], recv.at[slot]
        return pltpu.make_async_remote_copy(
            src_ref=src, dst_ref=dst, send_sem=send, recv_sem=recv, device_id={"tx": other}, device_id_type=MESH
        )

    peers = [lax.rem(me + d, n_tx) for d in range(1, n_tx)]
    code_refs = (code_out, code_in, code_send, code_recv)
    block_refs = (sent, landed, block_send, block_recv)
    strip_refs = (strip_out, strip_in, strip_send, strip_recv)
    for peer in peers:
        exchange(*code_refs, peer).start()
    for g, span in enumerate(spans):
        if g:
            pack(*span)
        else:
            for peer in peers:
                exchange(*block_refs, peer, g, span).start()
        landed[me, span[0] : span[1]] = sent[me, span[0] : span[1]]

    def halo(axis, src, dst, side, g, place_at, other, sending):
        span = slice(*spans[g])
        return pltpu.make_async_remote_copy(
            src_ref=src.at[side, span], dst_ref=dst.at[1 - side, span], send_sem=halo_send.at[g, place_at + side],
            recv_sem=halo_recv.at[g, place_at + 1 - side], device_id={axis: other}, device_id_type=MESH,
        )

    def swap(axis, at, n, src, dst, g, place_at):
        span = slice(*spans[g])

        @pl.when(at > 0)
        def _():
            halo(axis, src, dst, 0, g, place_at, at - 1, True).start()

        @pl.when(at < n - 1)
        def _():
            halo(axis, src, dst, 1, g, place_at, at + 1, True).start()

        @pl.when(at == 0)
        def _():
            dst[0, span] = jnp.zeros_like(dst[0, span])

        @pl.when(at == n - 1)
        def _():
            dst[1, span] = jnp.zeros_like(dst[1, span])

    def swapped(axis, at, n, src, dst, g, place_at):
        @pl.when(at > 0)
        def _():
            halo(axis, src, dst, 0, g, place_at, at - 1, True).wait_send()
            halo(axis, src, dst, 1, g, place_at, at - 1, False).wait_recv()

        @pl.when(at < n - 1)
        def _():
            halo(axis, src, dst, 1, g, place_at, at + 1, True).wait_send()
            halo(axis, src, dst, 0, g, place_at, at + 1, False).wait_recv()

    cols = ("ty", col, n_ty, cols_out, cols_in)
    line = ("tx", me, n_tx, rows_out, rows_in)
    landing = []

    def stage_a(g):
        first, last = spans[g]
        if g == 0:
            for peer in peers:
                exchange(*code_refs, peer, slot=peer).wait_recv()
            slot_id = lax.broadcasted_iota(jnp.int32, (SLOTS, 1), 0).astype(F32) + 1.0
            found = [jnp.where(slot_id == code_in[s][:1, :seats], 1.0, 0.0) for s in range(n_tx)]
            landing.append(jnp.concatenate(found * 2, axis=1).astype(BF))
        for peer in peers:
            exchange(*block_refs, peer, g, spans[g]).wait_send()
            if g + 1 < groups:
                exchange(*block_refs, peer, g + 1, spans[g + 1]).start()
        for peer in peers:
            exchange(*block_refs, peer, g, spans[g], slot=peer).wait_recv()
        cover = jnp.concatenate([landed[s, 0] for s in range(n_tx)], axis=0)
        wide = cover.astype(F32)
        for c in range(first, last):
            if c == 0:
                total = dot(landing[0][:, : n_tx * seats], cover)
            else:
                values = jnp.concatenate([landed[s, c] for s in range(n_tx)], axis=0).astype(F32)
                total = dot(landing[0], split(values * wide, 0))
            for half in range(2):
                part = total[:, half * TS : half * TS + TS].reshape(TS // BS, 8, TS)
                field[c, :, half] = regroup(part)
        for c in range(first, last):
            tile = field[c].reshape(TS, TS).T
            tiles[c] = tile
            if c == 0:
                for i in (0, 3, 6, 1, 2, 4, 5, 7, 8):
                    loads[i].wait()
            got = dot(dc[...], split(tile, 0, three=True))
            stack[c] = got[:TS]
            cols_out[0, c] = got[TS : TS + 8]
            cols_out[1, c] = got[TS + 8 : TS + 16]
        swap(*cols, g, 0)

    def stage_b(g):
        first, last = spans[g]
        swapped(*cols, g, 0)
        parts = []
        for c in range(first, last):
            whole = stack[c]
            parts += [whole[:8] + cols_in[0, c], whole[8:16] + cols_in[1, c], whole[16:]]
        flat = split(jnp.concatenate(parts, axis=0), 1, three=True)
        edges = lax.dot_general(de[...], flat, (((1,), (1,)), ((), ())), preferred_element_type=F32)
        for c in range(first, last):
            at = slice((c - first) * TS, (c - first + 1) * TS)
            rows_out[0, c] = edges[:8, at]
            rows_out[1, c] = edges[8:, at]
        swap(*line, g, 2)
        got = dot(flat, dr[...])
        for c in range(first, last):
            deep[c] = got[(c - first) * TS : (c - first + 1) * TS]

    def stage_c(g):
        first, last = spans[g]
        swapped(*line, g, 2)
        for c in range(first, last):
            rim = jnp.concatenate([rows_in[0, c], rows_in[1, c], jnp.zeros((TS - 16, TS), F32)], axis=0)
            deep[c] = deep[c] + rim.T
        if g == 0:
            ratio[0] = same[...] / (BACKGROUND + deep[0])
            ratio[1] = 1.0 / (BACKGROUND + tiles[0])
        mine = range(max(first, 1), last)
        whole = jnp.concatenate([deep[c] for c in mine], axis=0)
        detail = split(dot(split(whole, 1), pfr[...]), 1)
        bands = []
        finer = []
        for i, c in enumerate(mine):
            at = slice(i * TS, i * TS + TS)
            both = jnp.concatenate([detail[at, : 2 * TS], detail[at, 2 * TS :]], axis=0)
            bands.append((deep[c] - dot(pc[...], both[:, :TS])) * ratio[0])
            finer.append(dot(fc[...], both[:, TS:]))
        lifted = dot(split(jnp.concatenate(bands, axis=0), 1, three=True), qr[...])
        for i, c in enumerate(mine):
            at = slice(i * TS, i * TS + TS)
            final[i] = (tiles[c] - finer[i]) * ratio[1] + dot(qc[...], split(lifted[at], 0, three=True))
        for peer in peers:
            strip_out[g, peer] = strip_of(peer)
            exchange(*strip_refs, peer, g).start()
        strip_in[g, me] = strip_of(me)

    staged[...] = jnp.zeros_like(staged)

    def strip_of(t):
        for i in range(each):
            staged[i * strip : (i + 1) * strip, :] = final[i, pl.ds(t * strip, strip), :]
        return staged[...].astype(BF)

    for step in range(groups + 2):
        if step < groups:
            stage_a(step)
        if 0 < step <= groups:
            stage_b(step - 1)
        if step > 1:
            stage_c(step - 2)
    for g in range(groups):
        for peer in peers:
            exchange(*strip_refs, peer, g, slot=peer).wait_recv()
        for s in range(n_tx):
            got = strip_in[g, s].astype(F32)
            for i in range(each):
                out[g * each + i, 0, :, s * TS : (s + 1) * TS] = got[i * strip : (i + 1) * strip].astype(BF)
    for peer in peers:
        exchange(*code_refs, peer).wait_send()
        for g in range(groups):
            exchange(*strip_refs, peer, g).wait_send()


def solution(mesh):
    n_tx, n_ty = mesh.shape["tx"], mesh.shape["ty"]
    consts = tables()

    def local(scenes, cloud, destination, offset, counts):
        own = scenes.shape[2]
        chans = own + 1
        groups = 2 if own % 2 == 0 else 1
        each = own // groups
        spread = max(2, 2 * S_DEV // n_tx)
        seats = -(-spread // 16) * 16
        strip = TS // n_tx
        strip_rows = -(-each * strip // 16) * 16
        pixels = BS * BS
        vmem = pl.BlockSpec(memory_space=pltpu.VMEM)
        hbm = pl.BlockSpec(memory_space=pltpu.HBM)
        dma = pltpu.SemaphoreType.DMA
        return pl.pallas_call(
            functools.partial(kernel, n_tx, n_ty, own, groups, spread, seats, strip),
            out_shape=jax.ShapeDtypeStruct((own, 1, strip, TS * n_tx), BF),
            in_specs=[vmem] * 3 + [hbm] * 11,
            out_specs=vmem,
            scratch_shapes=[pltpu.VMEM(x.shape[1:], BF) for x in consts[:6]]
            + [pltpu.VMEM(x.shape, BF) for x in consts[6:8]]
            + [
                pltpu.VMEM((TS, TS), F32),
                pltpu.VMEM((own, S_DEV, pixels), BF),
                pltpu.VMEM((S_DEV, pixels), BF),
                pltpu.VMEM((n_tx, chans, seats, pixels), BF),
                pltpu.VMEM((n_tx, chans, seats, pixels), BF),
                pltpu.VMEM((n_tx, 8, TS), F32),
                pltpu.VMEM((n_tx, 8, TS), F32),
                pltpu.VMEM((chans, TS // BS, 2, 8, TS), F32),
                pltpu.VMEM((chans, TS, TS), F32),
                pltpu.VMEM((chans, TS, TS), F32),
                pltpu.VMEM((chans, TS, TS), F32),
                pltpu.VMEM((2, chans, 8, TS), F32),
                pltpu.VMEM((2, chans, 8, TS), F32),
                pltpu.VMEM((2, chans, 8, TS), F32),
                pltpu.VMEM((2, chans, 8, TS), F32),
                pltpu.VMEM((2, TS, TS), F32),
                pltpu.VMEM((each, TS, TS), F32),
                pltpu.VMEM((strip_rows, TS), F32),
                pltpu.VMEM((groups, n_tx, strip_rows, TS), BF),
                pltpu.VMEM((groups, n_tx, strip_rows, TS), BF),
                dma((9,)), dma((2,)),
                dma((groups, n_tx)), dma((groups, n_tx)), dma((n_tx,)), dma((n_tx,)),
                dma((groups, 4)), dma((groups, 4)), dma((groups, n_tx)), dma((groups, n_tx)),
            ],
            compiler_params=pltpu.CompilerParams(
                collective_id=0, has_side_effects=True, vmem_limit_bytes=62 * 1024 * 1024
            ),
        )(destination, offset, counts, jnp.swapaxes(scenes, 1, 2), cloud, *(jnp.asarray(x) for x in consts))

    placed = (
        P(("region", "ty"), "tx", "band", None),
        P(("region", "ty"), "tx", None),
        P(("region", "ty"), "tx"),
        P(("region", "ty"), "tx"),
        P(("region", "ty"), "tx"),
    )
    return jax.shard_map(
        local, mesh=mesh, in_specs=placed, out_specs=P("band", ("region", "ty"), "tx", None), check_vma=False
    )
```

```python
import functools

import jax
import jax.numpy as jnp
import ml_dtypes
import numpy as np
from jax import lax
from jax.experimental import pallas as pl
from jax.experimental.pallas import tpu as pltpu
from jax.sharding import PartitionSpec as P

TS = 128
BS = 16
S_DEV = 64
SLOTS = 64
TAPS = (0.0625, 0.25, 0.375, 0.25, 0.0625)
BACKGROUND = 0.25
MESH = pl.DeviceIdType.MESH
BF = jnp.bfloat16
F32 = jnp.float32
REACH = {1: (-1, 64), 2: (-1, 33), 3: (-1, 17)}


def stack_order():
    left, right, rest = [], [], []
    for level, (first, last) in REACH.items():
        width = 2 * (2**level - 1)
        for p in range(first, last + 1):
            entry = (level, p)
            if 2**level * p - width < 0:
                left.append(entry)
            elif 2**level * p + width >= TS:
                right.append(entry)
            else:
                rest.append(entry)
    assert len(left) == 8 and len(right) == 8 and len(rest) <= 112
    return left + right + rest


def operators(is_first, is_last):
    order = stack_order()
    low, high = (0 if is_first else -TS), (TS if is_last else 2 * TS)
    down = {0: np.eye(3 * TS)}
    begin = {0: -TS}
    for p in range(3 * TS):
        if not low <= p - TS < high:
            down[0][p] = 0
    for level in (1, 2, 3):
        extent = 3 * TS >> level
        begin[level] = -(TS >> level)
        matrix = np.zeros((extent, 3 * TS))
        for i in range(extent):
            p = begin[level] + i
            if not (low >> level) <= p < (high >> level):
                continue
            for a, tap in enumerate(TAPS):
                source = 2 * p + a - 2 - begin[level - 1]
                if 0 <= source < down[level - 1].shape[0]:
                    matrix[i] += tap * down[level - 1][source]
        down[level] = matrix
    where = {entry: i for i, entry in enumerate(order)}
    d = np.zeros((TS, 3 * TS))
    for (level, p), i in where.items():
        d[i] = down[level][p - begin[level]]

    def grown(p):
        half = p // 2
        if p % 2 == 0:
            return ((half - 1, 0.125), (half, 0.75), (half + 1, 0.125))
        return ((half, 0.5), (half + 1, 0.5))

    up = np.zeros((TS, TS))
    for (level, p), i in where.items():
        if level < 3 and (low >> level) <= p < (high >> level):
            for q, weight in grown(p):
                up[i, where[(level + 1, q)]] += weight
    f = np.zeros((TS, TS))
    for p in range(TS):
        for q, weight in grown(p):
            f[p, where[(1, q)]] += weight
    q = f @ (np.eye(TS) + up + up @ up)
    return d, up, f, q


def bf16(x):
    return x.astype(ml_dtypes.bfloat16)


def tables():
    order = stack_order()
    levels = np.array([level for level, _ in order] + [0] * (TS - len(order)))
    same = ((levels[:, None] == levels[None, :]) & (levels[:, None] > 0)).astype(np.float32)
    dc, pc, qc, dr, pfr, qr = [], [], [], [], [], []
    for variant in range(4):
        d, up, f, q = operators(variant % 2 == 1, variant >= 2)
        mid = operators(False, False)[0]
        to_left = mid[8:16, 2 * TS :]
        to_right = mid[0:8, :TS]
        edges = np.concatenate([to_left, to_right])
        own = np.concatenate([d[:, TS : 2 * TS], edges])
        top = bf16(own).astype(np.float64)
        low = own - top
        three = np.concatenate([top, top, low], axis=1)
        assert np.all(bf16(low).astype(np.float64) == low)
        assert np.all(bf16(up).astype(np.float64) == up)
        q_top = bf16(q).astype(np.float64)
        q_three = np.concatenate([q_top, q_top, q - q_top], axis=1)
        dc.append(three)
        dr.append(three[:TS].T)
        pc.append(np.concatenate([up, up], axis=1))
        qc.append(q_three)
        pf = np.concatenate([up.T, f.T], axis=1)
        pfr.append(np.concatenate([pf, pf], axis=0))
        qr.append(q_three.T)
    de = dc[0][TS:]
    fc = np.concatenate([f, f], axis=1)
    return [bf16(np.stack(x)) for x in (dc, pc, qc, dr, pfr, qr)] + [bf16(de), bf16(fc), same]


def split(x, axis, three=False):
    top = x.astype(BF)
    low = (x - top.astype(F32)).astype(BF)
    return jnp.concatenate([top, low, top] if three else [top, low], axis=axis)


def dot(a, b):
    return jnp.dot(a, b, preferred_element_type=F32)


def regroup(x):
    row = lax.broadcasted_iota(jnp.int32, x.shape, 1)
    col = lax.broadcasted_iota(jnp.int32, x.shape, 2) // BS
    for d in (4, 2, 1):
        row_bit, col_bit = (row // d) % 2, (col // d) % 2
        ahead = pltpu.roll(pltpu.roll(x, 8 - d, 1), BS * d, 2)
        if d == 4:
            x = jnp.where(row_bit == col_bit, x, ahead)
        else:
            behind = pltpu.roll(pltpu.roll(x, d, 1), TS - BS * d, 2)
            x = jnp.where(row_bit == col_bit, x, jnp.where(row_bit == 0, ahead, behind))
    return x


def kernel(
    n_tx, n_ty, own, groups, spread, seats, strip,
    destination, offset, counts, scenes_h, cloud_h, *refs,
):
    consts_h, refs = refs[:9], refs[9:]
    out, refs = refs[0], refs[1:]
    consts, refs = refs[:9], refs[9:]
    dc, pc, qc, dr, pfr, qr, de, fc, same = consts
    (scenes, cloud, sent, landed, code_out, code_in, field, tiles, stack, deep, cols_out, cols_in, rows_out, rows_in,
     ratio, final, staged, strip_out, strip_in,
     const_sem, in_sem, block_send, block_recv, code_send, code_recv, halo_send, halo_recv, strip_send, strip_recv) = refs
    me, col = lax.axis_index("tx"), lax.axis_index("ty")
    chans = own + 1
    pixels = BS * BS
    variant_c = jnp.where(col == 0, 1, 0) + jnp.where(col == n_ty - 1, 2, 0)
    variant_r = jnp.where(me == 0, 1, 0) + jnp.where(me == n_tx - 1, 2, 0)
    fetch = [
        pltpu.make_async_copy(scenes_h.at[0], scenes, in_sem.at[0]),
        pltpu.make_async_copy(cloud_h.at[0], cloud, in_sem.at[1]),
    ]
    for f in fetch:
        f.start()

    barrier = pltpu.get_barrier_semaphore()
    for d in range(1, n_tx):
        pl.semaphore_signal(barrier, inc=1, device_id={"tx": lax.rem(me + d, n_tx)}, device_id_type=MESH)

    @pl.when(col > 0)
    def _():
        pl.semaphore_signal(barrier, inc=1, device_id={"ty": col - 1}, device_id_type=MESH)

    @pl.when(col < n_ty - 1)
    def _():
        pl.semaphore_signal(barrier, inc=1, device_id={"ty": col + 1}, device_id_type=MESH)

    variants = [variant_c] * 3 + [variant_r] * 3 + [None] * 3
    loads = [
        pltpu.make_async_copy(src if v is None else src.at[v], dst, const_sem.at[i])
        for i, (src, dst, v) in enumerate(zip(consts_h, consts, variants))
    ]
    for load in loads:
        load.start()

    dest = jnp.broadcast_to(destination[...], (S_DEV, S_DEV))
    lane = lax.broadcasted_iota(jnp.int32, (S_DEV, S_DEV), 1)
    sub = lax.broadcasted_iota(jnp.int32, (S_DEV, S_DEV), 0)
    live = jnp.broadcast_to(counts[...], (S_DEV, S_DEV))
    earlier = (dest == dest.T) & (sub < lane)
    rank = jnp.sum(jnp.where(earlier, 1.0, 0.0), axis=0, keepdims=True)
    target = jnp.where(lane[:1] < live[:1], dest[:1].astype(F32) * seats + rank, -1.0)
    seat_id = lax.broadcasted_iota(jnp.int32, (n_tx * seats, 1), 0).astype(F32)
    chooser = jnp.where(seat_id == target, 1.0, 0.0).astype(BF)

    lanes = lax.broadcasted_iota(jnp.int32, (S_DEV, TS), 1)
    rank_t = jnp.broadcast_to(rank, (S_DEV, S_DEV)).T[:, :1]
    seat = jnp.where(lanes.astype(F32) == rank_t, 1.0, 0.0).astype(BF)
    tall = lax.broadcasted_iota(jnp.int32, (max(16, n_tx), S_DEV), 0)
    across = lax.broadcasted_iota(jnp.int32, tall.shape, 1)
    marks = jnp.where((tall == destination[...]) & (across < counts[...]), (offset[...] + 1).astype(F32), 0.0)
    codes = dot(marks.astype(BF), seat)
    for t in range(n_tx):
        code_out[t] = jnp.broadcast_to(codes[t : t + 1], (8, TS))
    code_in[me] = code_out[me]

    def pack(first, last):
        for c in range(first, last):
            got = dot(chooser, cloud[...] if c == 0 else scenes[c - 1]).astype(BF)
            sent[:, c] = got.reshape(n_tx, seats, pixels)

    for f in reversed(fetch):
        f.wait()
    each = own // groups
    spans = [(0 if g == 0 else 1 + g * each, 1 + (g + 1) * each) for g in range(groups)]
    pack(*spans[0])
    pl.semaphore_wait(barrier, n_tx - 1 + jnp.where(col > 0, 1, 0) + jnp.where(col < n_ty - 1, 1, 0))

    def exchange(src, dst, send, recv, other, g=None, span=None, slot=None):
        slot = me if slot is None else slot
        if span is not None:
            src, dst = src.at[other, span[0] : span[1]], dst.at[slot, span[0] : span[1]]
            send, recv = send.at[g, other], recv.at[g, slot]
        elif g is not None:
            src, dst, send, recv = src.at[g, other], dst.at[g, slot], send.at[g, other], recv.at[g, slot]
        else:
            src, dst, send, recv = src.at[other], dst.at[slot], send.at[other], recv.at[slot]
        return pltpu.make_async_remote_copy(
            src_ref=src, dst_ref=dst, send_sem=send, recv_sem=recv, device_id={"tx": other}, device_id_type=MESH
        )

    peers = [lax.rem(me + d, n_tx) for d in range(1, n_tx)]
    code_refs = (code_out, code_in, code_send, code_recv)
    block_refs = (sent, landed, block_send, block_recv)
    strip_refs = (strip_out, strip_in, strip_send, strip_recv)
    for peer in peers:
        exchange(*code_refs, peer).start()
    for g, span in enumerate(spans):
        if g:
            pack(*span)
        for peer in peers:
            exchange(*block_refs, peer, g, span).start()
        landed[me, span[0] : span[1]] = sent[me, span[0] : span[1]]

    def halo(axis, src, dst, side, g, place_at, other, sending):
        span = slice(*spans[g])
        return pltpu.make_async_remote_copy(
            src_ref=src.at[side, span], dst_ref=dst.at[1 - side, span], send_sem=halo_send.at[g, place_at + side],
            recv_sem=halo_recv.at[g, place_at + 1 - side], device_id={axis: other}, device_id_type=MESH,
        )

    def swap(axis, at, n, src, dst, g, place_at):
        span = slice(*spans[g])

        @pl.when(at > 0)
        def _():
            halo(axis, src, dst, 0, g, place_at, at - 1, True).start()

        @pl.when(at < n - 1)
        def _():
            halo(axis, src, dst, 1, g, place_at, at + 1, True).start()

        @pl.when(at == 0)
        def _():
            dst[0, span] = jnp.zeros_like(dst[0, span])

        @pl.when(at == n - 1)
        def _():
            dst[1, span] = jnp.zeros_like(dst[1, span])

    def swapped(axis, at, n, src, dst, g, place_at):
        @pl.when(at > 0)
        def _():
            halo(axis, src, dst, 0, g, place_at, at - 1, True).wait_send()
            halo(axis, src, dst, 1, g, place_at, at - 1, False).wait_recv()

        @pl.when(at < n - 1)
        def _():
            halo(axis, src, dst, 1, g, place_at, at + 1, True).wait_send()
            halo(axis, src, dst, 0, g, place_at, at + 1, False).wait_recv()

    cols = ("ty", col, n_ty, cols_out, cols_in)
    line = ("tx", me, n_tx, rows_out, rows_in)
    landing = []

    def stage_a(g):
        first, last = spans[g]
        if g == 0:
            for peer in peers:
                exchange(*code_refs, peer, slot=peer).wait_recv()
            slot_id = lax.broadcasted_iota(jnp.int32, (SLOTS, 1), 0).astype(F32) + 1.0
            found = [jnp.where(slot_id == code_in[s][:1, :seats], 1.0, 0.0) for s in range(n_tx)]
            landing.append(jnp.concatenate(found * 2, axis=1).astype(BF))
        for peer in peers:
            exchange(*block_refs, peer, g, spans[g]).wait_send()
        for peer in peers:
            exchange(*block_refs, peer, g, spans[g], slot=peer).wait_recv()
        cover = jnp.concatenate([landed[s, 0] for s in range(n_tx)], axis=0)
        wide = cover.astype(F32)
        for c in range(first, last):
            if c == 0:
                total = dot(landing[0][:, : n_tx * seats], cover)
            else:
                values = jnp.concatenate([landed[s, c] for s in range(n_tx)], axis=0).astype(F32)
                total = dot(landing[0], split(values * wide, 0))
            for half in range(2):
                part = total[:, half * TS : half * TS + TS].reshape(TS // BS, 8, TS)
                field[c, :, half] = regroup(part)
        for c in range(first, last):
            tile = field[c].reshape(TS, TS).T
            tiles[c] = tile
            if c == 0:
                for i in (0, 3, 6, 1, 2, 4, 5, 7, 8):
                    loads[i].wait()
            got = dot(dc[...], split(tile, 0, three=True))
            stack[c] = got[:TS]
            cols_out[0, c] = got[TS : TS + 8]
            cols_out[1, c] = got[TS + 8 : TS + 16]
        swap(*cols, g, 0)

    def stage_b(g):
        first, last = spans[g]
        swapped(*cols, g, 0)
        parts = []
        for c in range(first, last):
            whole = stack[c]
            parts += [whole[:8] + cols_in[0, c], whole[8:16] + cols_in[1, c], whole[16:]]
        flat = split(jnp.concatenate(parts, axis=0), 1, three=True)
        edges = lax.dot_general(de[...], flat, (((1,), (1,)), ((), ())), preferred_element_type=F32)
        for c in range(first, last):
            at = slice((c - first) * TS, (c - first + 1) * TS)
            rows_out[0, c] = edges[:8, at]
            rows_out[1, c] = edges[8:, at]
        swap(*line, g, 2)
        got = dot(flat, dr[...])
        for c in range(first, last):
            deep[c] = got[(c - first) * TS : (c - first + 1) * TS]

    def stage_c(g):
        first, last = spans[g]
        swapped(*line, g, 2)
        for c in range(first, last):
            rim = jnp.concatenate([rows_in[0, c], rows_in[1, c], jnp.zeros((TS - 16, TS), F32)], axis=0)
            deep[c] = deep[c] + rim.T
        if g == 0:
            ratio[0] = same[...] / (BACKGROUND + deep[0])
            ratio[1] = 1.0 / (BACKGROUND + tiles[0])
        mine = range(max(first, 1), last)
        whole = jnp.concatenate([deep[c] for c in mine], axis=0)
        detail = split(dot(split(whole, 1), pfr[...]), 1)
        bands = []
        finer = []
        for i, c in enumerate(mine):
            at = slice(i * TS, i * TS + TS)
            both = jnp.concatenate([detail[at, : 2 * TS], detail[at, 2 * TS :]], axis=0)
            bands.append((deep[c] - dot(pc[...], both[:, :TS])) * ratio[0])
            finer.append(dot(fc[...], both[:, TS:]))
        lifted = dot(split(jnp.concatenate(bands, axis=0), 1, three=True), qr[...])
        for i, c in enumerate(mine):
            at = slice(i * TS, i * TS + TS)
            final[i] = (tiles[c] - finer[i]) * ratio[1] + dot(qc[...], split(lifted[at], 0, three=True))
        for peer in peers:
            strip_out[g, peer] = strip_of(peer)
            exchange(*strip_refs, peer, g).start()
        strip_in[g, me] = strip_of(me)

    staged[...] = jnp.zeros_like(staged)

    def strip_of(t):
        for i in range(each):
            staged[i * strip : (i + 1) * strip, :] = final[i, pl.ds(t * strip, strip), :]
        return staged[...].astype(BF)

    for step in range(groups + 2):
        if step < groups:
            stage_a(step)
        if 0 < step <= groups:
            stage_b(step - 1)
        if step > 1:
            stage_c(step - 2)
    for g in range(groups):
        for peer in peers:
            exchange(*strip_refs, peer, g, slot=peer).wait_recv()
        for s in range(n_tx):
            got = strip_in[g, s].astype(F32)
            for i in range(each):
                out[g * each + i, 0, :, s * TS : (s + 1) * TS] = got[i * strip : (i + 1) * strip].astype(BF)
    for peer in peers:
        exchange(*code_refs, peer).wait_send()
        for g in range(groups):
            exchange(*strip_refs, peer, g).wait_send()


def solution(mesh):
    n_tx, n_ty = mesh.shape["tx"], mesh.shape["ty"]
    consts = tables()

    def local(scenes, cloud, destination, offset, counts):
        own = scenes.shape[2]
        chans = own + 1
        groups = 2 if own % 2 == 0 else 1
        each = own // groups
        spread = max(2, 2 * S_DEV // n_tx)
        seats = -(-spread // 16) * 16
        strip = TS // n_tx
        strip_rows = -(-each * strip // 16) * 16
        pixels = BS * BS
        vmem = pl.BlockSpec(memory_space=pltpu.VMEM)
        hbm = pl.BlockSpec(memory_space=pltpu.HBM)
        dma = pltpu.SemaphoreType.DMA
        return pl.pallas_call(
            functools.partial(kernel, n_tx, n_ty, own, groups, spread, seats, strip),
            out_shape=jax.ShapeDtypeStruct((own, 1, strip, TS * n_tx), BF),
            in_specs=[vmem] * 3 + [hbm] * 11,
            out_specs=vmem,
            scratch_shapes=[pltpu.VMEM(x.shape[1:], BF) for x in consts[:6]]
            + [pltpu.VMEM(x.shape, BF) for x in consts[6:8]]
            + [
                pltpu.VMEM((TS, TS), F32),
                pltpu.VMEM((own, S_DEV, pixels), BF),
                pltpu.VMEM((S_DEV, pixels), BF),
                pltpu.VMEM((n_tx, chans, seats, pixels), BF),
                pltpu.VMEM((n_tx, chans, seats, pixels), BF),
                pltpu.VMEM((n_tx, 8, TS), F32),
                pltpu.VMEM((n_tx, 8, TS), F32),
                pltpu.VMEM((chans, TS // BS, 2, 8, TS), F32),
                pltpu.VMEM((chans, TS, TS), F32),
                pltpu.VMEM((chans, TS, TS), F32),
                pltpu.VMEM((chans, TS, TS), F32),
                pltpu.VMEM((2, chans, 8, TS), F32),
                pltpu.VMEM((2, chans, 8, TS), F32),
                pltpu.VMEM((2, chans, 8, TS), F32),
                pltpu.VMEM((2, chans, 8, TS), F32),
                pltpu.VMEM((2, TS, TS), F32),
                pltpu.VMEM((each, TS, TS), F32),
                pltpu.VMEM((strip_rows, TS), F32),
                pltpu.VMEM((groups, n_tx, strip_rows, TS), BF),
                pltpu.VMEM((groups, n_tx, strip_rows, TS), BF),
                dma((9,)), dma((2,)),
                dma((groups, n_tx)), dma((groups, n_tx)), dma((n_tx,)), dma((n_tx,)),
                dma((groups, 4)), dma((groups, 4)), dma((groups, n_tx)), dma((groups, n_tx)),
            ],
            compiler_params=pltpu.CompilerParams(
                collective_id=0, has_side_effects=True, vmem_limit_bytes=62 * 1024 * 1024
            ),
        )(destination, offset, counts, jnp.swapaxes(scenes, 1, 2), cloud, *(jnp.asarray(x) for x in consts))

    placed = (
        P(("region", "ty"), "tx", "band", None),
        P(("region", "ty"), "tx", None),
        P(("region", "ty"), "tx"),
        P(("region", "ty"), "tx"),
        P(("region", "ty"), "tx"),
    )
    return jax.shard_map(
        local, mesh=mesh, in_specs=placed, out_specs=P("band", ("region", "ty"), "tx", None), check_vma=False
    )
```
